32 devices in a mesh: img: 8 (over z, x), pose: 4 (over y, core).
Axes of the slice: x: 2, y: 2, z: 4, core: 2. Of those that a mesh axis runs over, the one named last changes fastest.
Arguments:
- images: bfloat16 [2048, 4096], P('img'), may hold values from -100 to 100
- inv_noise: float32 [2048], P('img'), may hold values from 0.5 to 2
- defocus_class: int32 [2048], P('img'), may hold values from 0 to 15
- defocus: float32 [16], replicated, may hold values from 1 to 3
- pose_dir: int32 [512], P('pose'), may hold values from 0 to 503
- pose_shift: int32 [512, 2], P('pose'), may hold values from -8 to 8
- slabs: float32 [64, 4096], P('img', 'pose'), may hold values from -0.5 to 0.5
Outputs:
- slabs_out: float32 [64, 4096], P('img', 'pose')
- evidence: float32 [2048], P(('img', 'pose'))
The draws below stay inside these ranges and needn't reach their ends.
All inputs are finite; a program needn't handle non-finite values.
Results may differ from the reference program's by a relative error of at most 0.0027.
Values sent between devices are 32-bit elements; how exact they have to be, the bound alone decides.
A program may use at most 64 MiB of HBM per device.

```python
import math
import jax
import jax.numpy as jnp
from jax import lax

NS = 64
KW = 64
KH = 32
F = 4096
CLASSES = 16
STEPS = 2
IMG_DEV = 256
POSES = 512
IMAGES = 2048


def draw_inv_noise(key, part):
    uniform_values = jax.random.uniform(key, (IMAGES,), jnp.float32)
    lowest = jnp.log(0.5)
    highest = jnp.log(1.4)
    return jnp.exp(lowest + uniform_values * (highest - lowest)).astype(jnp.float32)


def draw_images(key, part):
    base_key = jax.random.fold_in(key, 11)
    level_key = jax.random.fold_in(key, 12)
    values = jnp.clip(jax.random.normal(base_key, (IMAGES, F), jnp.float32), -6.0, 6.0)
    level = jax.random.randint(level_key, (IMAGES,), 0, 3)
    strength = 8.0 + 4.0 * level.astype(jnp.float32)
    rows = jnp.arange(IMAGES, dtype=jnp.int32)
    factor = jnp.where(rows % 16 == 5, strength, 1.0 + 0.0 * strength)
    return (values * factor[:, None]).astype(jnp.bfloat16)


def set_ends(values, key, least, top_value):
    extent = values.shape
    spot = [jax.random.randint(jax.random.fold_in(key, axis), (), 0, extent[axis]) for axis in range(len(extent))]
    values = values.at[tuple(spot)].set(least)
    longest = extent.index(max(extent))
    spot[longest] = (spot[longest] + 1) % extent[longest]
    return values.at[tuple(spot)].set(top_value)


def steps_of(own_key, dims, cuts, low, top_value):
    def one(dim, parts):
        heights = jax.random.uniform(jax.random.fold_in(jax.random.fold_in(own_key, 6), dim), (parts,), jnp.float32, low / len(cuts), top_value / len(cuts))
        return jnp.repeat(jnp.exp(heights), dims[dim] // parts).reshape((-1,) + (1,) * (len(dims) - dim - 1))

    loudness = one(*cuts[0])
    for cut in cuts[1:]:
        loudness = loudness * one(*cut)
    return loudness


def noise(key, shape, scale, most, shards=(), held_as=jnp.bfloat16):
    drawn = scale * jax.random.normal(key, shape, jnp.float32)
    if shards:
        drawn = drawn * steps_of(key, shape, shards, -0.22, 0.18)
    return jnp.clip(drawn, -most, most).astype(held_as)


def setup_inputs(seed: int = 0) -> dict:
    keys = jax.random.split(jax.random.key(seed), 8)
    return {
        "images": draw_images(jax.random.fold_in(keys[7], 71), 0),
        "inv_noise": draw_inv_noise(jax.random.fold_in(keys[7], 71), 0),
        "defocus_class": set_ends(jax.random.randint(keys[2], (IMAGES,), 0, CLASSES), jax.random.fold_in(keys[2], 1), 0, CLASSES - 1).astype(jnp.int32),
        "defocus": jnp.clip(jnp.exp(jax.random.uniform(keys[3], (CLASSES,), jnp.float32, math.log(1.0), math.log(3.0))), 1.0, 3.0),
        "pose_dir": set_ends(jax.random.randint(keys[4], (POSES,), 0, 8 * (NS - 1)), jax.random.fold_in(keys[4], 1), 0, (8 * (NS - 1)) - 1).astype(jnp.int32),
        "pose_shift": set_ends(jax.random.randint(keys[5], (POSES, 2), -8, 9), jax.random.fold_in(keys[5], 1), -8, 8).astype(jnp.int32),
        "slabs": noise(keys[6], (NS, F), (6.0 * F ** -0.5), 0.5, ((0, 8), (1, 4)), jnp.float32),
    }


highest_precision = lax.Precision.HIGHEST

def coefficient_freqs():
    position = jnp.arange(KW * KH, dtype=jnp.int32)
    freq_x = (position % KW - KW // 2).astype(jnp.float32)
    freq_y = (position // KW).astype(jnp.float32)
    return (freq_x, freq_y)

def ctf_values(defocus):
    freq_x, freq_y = coefficient_freqs()
    radius_sq = (freq_x * freq_x + freq_y * freq_y) / (KH * KH)
    transfer = -jnp.sin(8.0 * defocus[:, None] * radius_sq[None, :] + 0.1)
    return jnp.concatenate([transfer, transfer], axis=1)

def slab_weights(pose_dir):
    lower = pose_dir // 8
    fraction = (pose_dir % 8).astype(jnp.float32) / 8.0
    slab_ids = jnp.arange(NS, dtype=jnp.int32)
    first = jnp.where(slab_ids[None, :] == lower[:, None], 1.0 - fraction[:, None], 0.0 * fraction[:, None])
    second = jnp.where(slab_ids[None, :] == lower[:, None] + 1, fraction[:, None], 0.0 * fraction[:, None])
    return first + second

def rotate(values, pose_shift, direction):
    freq_x, freq_y = coefficient_freqs()
    shift_x = pose_shift[:, 0:1].astype(jnp.float32)
    shift_y = pose_shift[:, 1:2].astype(jnp.float32)
    angles = 2.0 * math.pi / (4 * KH) * (shift_x * freq_x[None, :] + shift_y * freq_y[None, :])
    cosine = jnp.cos(angles)
    sine = direction * jnp.sin(angles)
    half_width = KW * KH
    real_part = values[:, :half_width]
    imag_part = values[:, half_width:]
    return jnp.concatenate([real_part * cosine - imag_part * sine, real_part * sine + imag_part * cosine], axis=1)

def class_table(defocus_class):
    return (defocus_class[:, None] == jnp.arange(CLASSES, dtype=jnp.int32)[None, :]).astype(jnp.float32)

def weight_images(images, class_onehot, table):
    image_ctf = jnp.dot(class_onehot, table, precision=highest_precision, preferred_element_type=jnp.float32)
    return image_ctf * images.astype(jnp.float32)

def tile_scores(references, weighted, ctf_sq, class_onehot, inv_noise):
    ref_sq = references * references
    energy = lax.dot_general(ctf_sq, ref_sq, (((1,), (1,)), ((), ())), precision=highest_precision, preferred_element_type=jnp.float32)
    picked = jnp.dot(class_onehot, energy, precision=highest_precision, preferred_element_type=jnp.float32)
    inner = lax.dot_general(weighted, references, (((1,), (1,)), ((), ())), precision=highest_precision, preferred_element_type=jnp.float32)
    return inv_noise[:, None] * (inner - 0.5 * picked)

def pose_pull(scores, inv_noise, weighted, class_onehot):
    peak = lax.optimization_barrier(jnp.max(scores, axis=1, keepdims=True))
    log_total = peak[:, 0] + jnp.log(lax.optimization_barrier(jnp.sum(jnp.exp(scores - peak), axis=1)))
    usage = (inv_noise[:, None] * jnp.exp(scores - log_total[:, None])).astype(jnp.bfloat16)
    pull = lax.dot_general(usage.astype(jnp.float32), weighted, (((0,), (0,)), ((), ())), precision=highest_precision, preferred_element_type=jnp.float32)
    mass = lax.dot_general(usage, class_onehot.astype(jnp.bfloat16), (((0,), (0,)), ((), ())), preferred_element_type=jnp.float32)
    return (log_total, pull, mass)

def slab_gradient(weights_mat, plain, pull, mass, pose_shift, ctf_sq):
    damping = jnp.dot(mass, ctf_sq, precision=highest_precision, preferred_element_type=jnp.float32)
    backward = rotate(pull, pose_shift, -1.0) - plain * damping
    return lax.dot_general(weights_mat, backward, (((0,), (0,)), ((), ())), precision=highest_precision, preferred_element_type=jnp.float32)

def reference(images, inv_noise, defocus_class, defocus, pose_dir, pose_shift, slabs):
    table = ctf_values(defocus)
    ctf_sq = table * table
    weights_mat = slab_weights(pose_dir)
    block_count = images.shape[0] // IMG_DEV
    image_blocks = images.reshape(block_count, IMG_DEV, F)
    noise_blocks = inv_noise.reshape(block_count, IMG_DEV)
    class_blocks = defocus_class.reshape(block_count, IMG_DEV)
    slab_map = slabs
    evidence = jnp.zeros((block_count, IMG_DEV), jnp.float32)
    for step_index in range(STEPS):
        plain = jnp.dot(weights_mat, slab_map, precision=highest_precision, preferred_element_type=jnp.float32)
        references = rotate(plain, pose_shift, 1.0)

        def visit(carry, block):
            block_images, block_noise, block_class = block
            onehot = class_table(block_class)
            weighted = weight_images(block_images, onehot, table)
            scores = tile_scores(references, weighted, ctf_sq, onehot, block_noise)
            log_total, pull, mass = pose_pull(scores, block_noise, weighted, onehot)
            return ((carry[0] + pull, carry[1] + mass), log_total)
        start_carry = (jnp.zeros((POSES, F), jnp.float32), jnp.zeros((POSES, CLASSES), jnp.float32))
        (pull, mass), evidence = lax.scan(visit, start_carry, (image_blocks, noise_blocks, class_blocks))
        gradient = slab_gradient(weights_mat, plain, pull, mass, pose_shift, ctf_sq)
        spread = jnp.sqrt(jnp.mean(gradient * gradient) + 1e-06)
        slab_map = slab_map + 0.05 * gradient / spread
    return (slab_map, evidence.reshape(-1))
```

```python
import functools
import math

import jax
import jax.numpy as jnp
from jax import lax
from jax.experimental import pallas as pl
from jax.experimental.pallas import tpu as pltpu
from jax.sharding import PartitionSpec as P

NS = 64
KW = 64
KH = 32
F = KW * KH * 2
CLASSES = 16
STEPS = 2
BW = 256
NB = F // BW
HB = NB // 2
F32 = jnp.float32
BF = jnp.bfloat16
MESH = pl.DeviceIdType.MESH


def dot(a, b):
    return jnp.dot(a, b, preferred_element_type=F32)


def dot_t(a, b):
    return lax.dot_general(a, b, (((1,), (1,)), ((), ())), preferred_element_type=F32)


def split2(v):
    hi = v.astype(BF)
    lo = (v - hi.astype(F32)).astype(BF)
    return hi, lo


def split3(v):
    hi = v.astype(BF)
    rest = v - hi.astype(F32)
    mid = rest.astype(BF)
    lo = (rest - mid.astype(F32)).astype(BF)
    return hi, mid, lo


def kernel(
    dims,
    img_ref, noise_ref, class_ref, defocus_ref, dir_ref, shift_ref, slab_ref,
    out_ref, ev_ref,
    wh, wl, cosr, sinr, csq, plain, m0, m1, grad, ra, s1, rb, s2, rc, own,
    ebuf, ta, tb, tc, sc_acc, en_acc, use_ref, mass_ref,
    ag_s, ag_r, rs_s, rs_r, ev_s, ev_r, t_s, t_r,
):
    (X, Z, U, R, K, KC) = dims
    KB = K // KC
    NI = img_ref.shape[0]
    NP = dir_ref.shape[1]
    NPOSE = 2 * U
    i = lax.axis_index("img")
    p = lax.axis_index("pose")
    z, x = lax.div(i, X), lax.rem(i, X)
    u, c = lax.div(p, 2), lax.rem(p, 2)

    def coords(off):
        dz, dx, du, dc = off
        return (lax.rem(z + dz, Z), lax.rem(x + dx, X), lax.rem(u + du, U), lax.rem(c + dc, 2))

    def device(co):
        return (co[0] * X + co[1], co[2] * 2 + co[3])

    offs_a = [(0, 0, 0, 1)]
    offs_b = [(0, dx, du, 0) for du in range(U) for dx in range(X) if du or dx]
    offs_c = [(dz, 0, 0, 0) for dz in range(1, Z)]
    offs_e = [(0, 0, du, dc) for du in range(U) for dc in range(2) if du or dc]
    everyone = sorted(set(offs_a + offs_b + offs_c + offs_e))
    nb, nc = len(offs_b), len(offs_c)

    barrier = pltpu.get_barrier_semaphore()
    for off in everyone:
        pl.semaphore_signal(barrier, inc=1, device_id=device(coords(off)), device_id_type=MESH)
    pl.semaphore_wait(barrier, len(everyone))

    def send(src, dst, ss, rs, off):
        d = pltpu.make_async_remote_copy(
            src_ref=src, dst_ref=dst, send_sem=ss, recv_sem=rs,
            device_id=device(coords(off)), device_id_type=MESH,
        )
        d.start()
        return d

    pend = []

    def gather_start(m, g):
        return [
            send(m.at[c, :, u, x, z], m.at[c, :, u, x, z], ag_s.at[g, n], ag_r.at[g, n], off)
            for n, off in enumerate(offs_c)
        ]

    def gather_b(m, g, first):
        for d in first:
            d.wait_recv()
        pend.extend(first)
        return [
            send(m.at[c, :, u, x], m.at[c, :, u, x], ag_s.at[g, nc + n], ag_r.at[g, nc + n], off)
            for n, off in enumerate(offs_b)
        ]

    def gather_a(m, g, second):
        for d in second:
            d.wait_recv()
        pend.extend(second)
        return send(m.at[c], m.at[c], ag_s.at[g, nc + nb], ag_r.at[g, nc + nb], offs_a[0])

    for k in range(K):
        m0[c, k, u, x, z] = slab_ref[:, k * BW:(k + 1) * BW]
    first = gather_start(m0, 0)

    row_r = lax.broadcasted_iota(jnp.int32, (128, NI), 0)
    class_row = class_ref[...]
    hot = jnp.where(row_r % CLASSES == class_row, 1.0, 0.0)
    hot3 = jnp.where(row_r < 3 * CLASSES, hot, 0.0)
    pick = jnp.where((row_r < CLASSES) | ((row_r >= 2 * CLASSES) & (row_r < 3 * CLASSES)), hot, 0.0).astype(BF)
    hot3_t = hot3.T.astype(BF)

    srow = lax.broadcasted_iota(jnp.int32, (128, NP), 0)
    sx_ = lax.div(srow, Z * R)
    sz_ = lax.rem(lax.div(srow, R), Z)
    slab_id = jnp.where(srow < NS, (sz_ * X + sx_) * R + lax.rem(srow, R), -5)
    pdir = dir_ref[...]
    lower = lax.div(pdir, 8)
    frac = lax.rem(pdir, 8).astype(F32) / 8.0
    wt = jnp.where(slab_id == lower, 1.0 - frac, 0.0) + jnp.where(slab_id == lower + 1, frac, 0.0)
    w_t = wt[:NS].astype(BF)
    w_t2 = jnp.concatenate([w_t, w_t], axis=1)
    w = wt.T[:, :NS]
    w3 = jnp.concatenate([w, w, w], axis=1).astype(BF)

    first = gather_b(m0, 0, first)

    lane = lax.broadcasted_iota(jnp.int32, (NP, 128), 1)
    shx = shift_ref[:, 0:1]
    shy = shift_ref[:, 1:2]
    turn = 2.0 * math.pi / (4 * KH)
    base = turn * (shx * (lane % KW - KW // 2) + shy * lax.div(lane, KW)).astype(F32)
    inc = turn * (2 * shy + 0 * lane).astype(F32)
    cb, sb, ci, si = jnp.cos(base), jnp.sin(base), jnp.cos(inc), jnp.sin(inc)
    for t in range(KW * KH // 128):
        b, h = (t * 128) // BW, (t * 128) % BW
        cosr[b, :, h:h + 128] = cb
        sinr[b, :, h:h + 128] = sb
        cb, sb = cb * ci - sb * si, sb * ci + cb * si

    for b in range(HB):
        pos = lax.broadcasted_iota(jnp.int32, (CLASSES, BW), 1) + b * BW
        fx = (pos % KW - KW // 2).astype(F32)
        fy = lax.div(pos, KW).astype(F32)
        rad = (fx * fx + fy * fy) / (KH * KH)
        tab = -jnp.sin(8.0 * defocus_ref[...] * rad + 0.1)
        zero = jnp.zeros((128 - 3 * CLASSES, BW), BF)
        hi, lo = split2(tab * tab)
        csq[b] = jnp.concatenate([hi, hi, lo, zero], axis=0)
        t1, t2, t3 = split3(tab)
        sel = dot(hot3_t, jnp.concatenate([t1, t2, t3, zero], axis=0))
        for bb in (b, b + HB):
            v = sel * img_ref[:, bb * BW:(bb + 1) * BW].astype(F32)
            hi, lo = split2(v)
            wh[bb] = hi
            wl[bb] = lo
    last = gather_a(m0, 0, first)
    last.wait_recv()
    pend.append(last)

    def place(b):
        q = lax.div(b, K)
        return lax.rem(q, 2), lax.rem(b, K), lax.div(q, 2)

    def rows_of(m, cc, k, uu):
        return jnp.concatenate([m[cc, k, uu, n // Z, n % Z] for n in range(X * Z)], axis=0)

    noise = noise_ref[...]

    for step in range(STEPS):
        sc_acc[...] = jnp.zeros_like(sc_acc)
        en_acc[...] = jnp.zeros_like(en_acc)

        def forward(b, carry):
            cc, k, uu = place(b)
            part = []
            for half in range(2):
                rows = rows_of(m0, cc, k, uu + half * (U // 2))
                v = dot(w3, jnp.concatenate(split3(rows), axis=0))
                plain[b + half * HB] = v
                part.append(v)
            re, im = part
            power = re * re + im * im
            hi, lo = split2(power)
            en_acc[...] += dot_t(hi, csq[b]) + dot_t(lo, csq[b])
            co, si_ = cosr[b], sinr[b]
            for half, v in enumerate((re * co - im * si_, re * si_ + im * co)):
                rh, rl = split2(v)
                bb = b + half * HB
                both = dot_t(jnp.concatenate([rh, rl], axis=0), wh[bb])
                sc_acc[...] += both[:NP] + both[NP:] + dot_t(rh, wl[bb])
            return carry

        lax.fori_loop(0, HB, forward, 0)
        e1, e2, e3 = split3(en_acc[...])
        picked = dot(e1, pick) + dot(e2, pick) + dot(e3, pick)
        scores = noise * (sc_acc[...] - 0.5 * picked)
        lpeak = jnp.max(scores, axis=0, keepdims=True)
        lsum = jnp.sum(jnp.exp(scores - lpeak), axis=0, keepdims=True)
        ebuf[step, p] = jnp.concatenate([lpeak, lsum, jnp.zeros((6, NI), F32)], axis=0)
        sent = [
            send(ebuf.at[step, p], ebuf.at[step, p], ev_s.at[step, n], ev_r.at[step, n], off)
            for n, off in enumerate(offs_e)
        ]
        for d in sent:
            d.wait()
        peak = lpeak
        for n in range(NPOSE):
            peak = jnp.maximum(peak, ebuf[step, n, 0:1, :])
        total = jnp.zeros_like(peak)
        for n in range(NPOSE):
            total += ebuf[step, n, 1:2, :] * jnp.exp(ebuf[step, n, 0:1, :] - peak)
        log_total = peak + jnp.log(total)
        usage = (noise * jnp.exp(scores - log_total)).astype(BF)
        use_ref[...] = usage
        mass = dot(usage, hot3_t)
        mh, ml = split2(mass)
        mcol = lax.broadcasted_iota(jnp.int32, mass.shape, 1)
        mass_ref[...] = jnp.where((mcol < CLASSES) | (mcol >= 2 * CLASSES), mh.astype(F32), ml.astype(F32)).astype(BF)

        def backward(cc, kc):
            def body(t, carry):
                k = kc * KB + lax.div(t, U // 2)
                uu = lax.rem(t, U // 2)
                b = (2 * uu + cc) * K + k
                use = use_ref[...]
                pr = dot(use, wh[b]) + dot(use, wl[b])
                pi = dot(use, wh[b + HB]) + dot(use, wl[b + HB])
                damp = dot(mass_ref[...], csq[b])
                co, si_ = cosr[b], sinr[b]
                outs = (
                    pr * co + pi * si_ - plain[b] * damp,
                    pi * co - pr * si_ - plain[b + HB] * damp,
                )
                for half, v in enumerate(outs):
                    hi, lo = split2(v)
                    g = dot(w_t2, jnp.concatenate([hi, lo], axis=0))
                    for n in range(X * Z):
                        grad[step, cc, k, uu + half * (U // 2), n // Z, n % Z] = g[n * R:(n + 1) * R]
                return carry

            lax.fori_loop(0, KB * (U // 2), body, 0)

        per = 1 + nb + nc
        oc = lax.rem(c + 1, 2)
        stage = []
        for kc in range(KC):
            backward(oc, kc)
            ks = pl.ds(kc * KB, KB)
            stage.append(send(grad.at[step, oc, ks], ra.at[step, ks],
                              rs_s.at[step, kc * per], rs_r.at[step, kc * per], offs_a[0]))
        slot = u * X + x
        stage_b = []
        for kc in range(KC):
            backward(c, kc)
            stage[kc].wait_recv()
            ks = pl.ds(kc * KB, KB)
            for k in range(kc * KB, (kc + 1) * KB):
                s1[step, k] = grad[step, c, k] + ra[step, k]
            ds = []
            for n, off in enumerate(offs_b):
                _, xx, uu, _ = coords(off)
                ds.append(send(s1.at[step, ks, uu, xx], rb.at[step, slot, ks],
                               rs_s.at[step, kc * per + 1 + n], rs_r.at[step, kc * per + 1 + n], off))
            rb[step, slot, ks] = s1[step, ks, u, x]
            stage_b.append(ds)
        stage_c = []
        for kc in range(KC):
            for d in stage_b[kc]:
                d.wait_recv()
            ks = pl.ds(kc * KB, KB)
            tot = rb[step, 0, ks]
            for n in range(1, U * X):
                tot += rb[step, n, ks]
            s2[step, ks] = tot
            ds = []
            for n, off in enumerate(offs_c):
                zz = coords(off)[0]
                ds.append(send(s2.at[step, ks, zz], rc.at[step, z, ks],
                               rs_s.at[step, kc * per + 1 + nb + n], rs_r.at[step, kc * per + 1 + nb + n], off))
            rc[step, z, ks] = s2[step, ks, z]
            stage_c.append(ds)
        for kc in range(KC):
            for d in stage_c[kc]:
                d.wait_recv()
            ks = pl.ds(kc * KB, KB)
            tot = rc[step, 0, ks]
            for n in range(1, Z):
                tot += rc[step, n, ks]
            own[ks] = tot
        pend.extend(stage)
        for ds in stage_b + stage_c:
            pend.extend(ds)

        if step < STEPS - 1:
            m1[c, :, u, x, z] = own[...]
            first = gather_start(m1, 1)
            first = gather_b(m1, 1, first)
            last = gather_a(m1, 1, first)
            last.wait_recv()
            pend.append(last)
            sq = jnp.zeros((R, BW), F32)
            for cc in range(2):
                for k in range(K):
                    for uu in range(U):
                        for n in range(X * Z):
                            v = m1[cc, k, uu, n // Z, n % Z]
                            sq += v * v
            spread = jnp.sqrt(jnp.sum(sq, keepdims=True) / (NS * F) + 1e-06)
            for d in pend:
                d.wait_send()
            pend.clear()
            for cc in range(2):
                for k in range(K):
                    for uu in range(U):
                        for n in range(X * Z):
                            at = (cc, k, uu, n // Z, n % Z)
                            m0[at] = m0[at] + 0.05 * m1[at] / spread
        else:
            g = own[...]
            mine = jnp.sum(jnp.sum(g * g, axis=0), keepdims=True)
            ta[c] = mine + jnp.zeros((8, 128), F32)
            d = send(ta.at[c], ta.at[c], t_s.at[0], t_r.at[0], offs_a[0])
            d.wait()
            tb[slot] = ta[0] + ta[1]
            ds = [send(tb.at[slot], tb.at[slot], t_s.at[1 + n], t_r.at[1 + n], off) for n, off in enumerate(offs_b)]
            for d in ds:
                d.wait()
            tot = tb[0]
            for n in range(1, U * X):
                tot += tb[n]
            tc[z] = tot
            ds = [send(tc.at[z], tc.at[z], t_s.at[1 + nb + n], t_r.at[1 + nb + n], off) for n, off in enumerate(offs_c)]
            for d in ds:
                d.wait()
            tot = tc[0]
            for n in range(1, Z):
                tot += tc[n]
            spread = jnp.sqrt(tot[0:1, 0:1] / (NS * F) + 1e-06)
            for k in range(K):
                out_ref[:, k * BW:(k + 1) * BW] = m0[c, k, u, x, z] + 0.05 * own[k] / spread
            share = NI // NPOSE
            ev = jnp.zeros((1, share), F32)
            for n in range(NPOSE):
                ev = jnp.where(p == n, log_total[:, n * share:(n + 1) * share], ev)
            ev_ref[...] = ev
    for d in pend:
        d.wait_send()


def shards(dims, images, inv_noise, defocus_class, defocus, pose_dir, pose_shift, slabs):
    X, Z, U, R, K, KC = dims
    ni, np_ = images.shape[0], pose_dir.shape[0]
    C = slabs.shape[1]
    npose = 2 * U
    nb, nc = U * X - 1, Z - 1
    vm = pltpu.VMEM
    dma = pltpu.SemaphoreType.DMA
    whole = (2, K, U, X, Z, R, BW)
    per = 1 + nb + nc
    scratch = [
        vm((NB, ni, BW), BF), vm((NB, ni, BW), BF),
        vm((HB, np_, BW), F32), vm((HB, np_, BW), F32),
        vm((HB, 128, BW), BF),
        vm((NB, np_, BW), F32),
        vm(whole, F32), vm(whole, F32),
        vm((STEPS,) + whole, F32),
        vm((STEPS,) + whole[1:], F32), vm((STEPS,) + whole[1:], F32),
        vm((STEPS, U * X, K, Z, R, BW), F32),
        vm((STEPS, K, Z, R, BW), F32),
        vm((STEPS, Z, K, R, BW), F32),
        vm((K, R, BW), F32),
        vm((STEPS, npose, 8, ni), F32),
        vm((2, 8, 128), F32), vm((U * X, 8, 128), F32), vm((Z, 8, 128), F32),
        vm((np_, ni), F32), vm((np_, 128), F32),
        vm((np_, ni), BF), vm((np_, 128), BF),
        dma((2, per)), dma((2, per)),
        dma((STEPS, KC * per)), dma((STEPS, KC * per)),
        dma((STEPS, npose)), dma((STEPS, npose)),
        dma((per,)), dma((per,)),
    ]
    out, ev = pl.pallas_call(
        functools.partial(kernel, dims),
        out_shape=(
            jax.ShapeDtypeStruct(slabs.shape, F32),
            jax.ShapeDtypeStruct((1, ni // npose), F32),
        ),
        in_specs=[pl.BlockSpec(memory_space=vm)] * 7,
        out_specs=(pl.BlockSpec(memory_space=vm),) * 2,
        scratch_shapes=scratch,
        compiler_params=pltpu.CompilerParams(
            collective_id=0, has_side_effects=True, vmem_limit_bytes=56 * 1024 * 1024
        ),
        cost_estimate=pl.CostEstimate(flops=8 * ni * np_ * F, bytes_accessed=2 * ni * F, transcendentals=0),
    )(
        images, inv_noise[None, :], defocus_class[None, :], defocus[:, None],
        pose_dir[None, :], pose_shift, slabs,
    )
    return out, ev[0]


def solution(mesh):
    n_img, n_pose = mesh.shape["img"], mesh.shape["pose"]
    X, Z, U = 2, n_img // 2, n_pose // 2
    R = NS // n_img
    K = F // n_pose // BW
    KC = 2 if K % 2 == 0 else 1
    in_specs = (
        P("img", None),
        P("img"),
        P("img"),
        P(),
        P("pose"),
        P("pose", None),
        P("img", "pose"),
    )
    out_specs = (P("img", "pose"), P(("img", "pose")))
    body = functools.partial(shards, (X, Z, U, R, K, KC))
    return jax.shard_map(body, mesh=mesh, in_specs=in_specs, out_specs=out_specs, check_vma=False)
```

```python
import functools
import math

import jax
import jax.numpy as jnp
from jax import lax
from jax.experimental import pallas as pl
from jax.experimental.pallas import tpu as pltpu
from jax.sharding import PartitionSpec as P

NS = 64
KW = 64
KH = 32
F = KW * KH * 2
CLASSES = 16
STEPS = 2
BW = 256
NB = F // BW
HB = NB // 2
F32 = jnp.float32
BF = jnp.bfloat16
MESH = pl.DeviceIdType.MESH


def dot(a, b):
    return jnp.dot(a, b, preferred_element_type=F32)


def dot_t(a, b):
    return lax.dot_general(a, b, (((1,), (1,)), ((), ())), preferred_element_type=F32)


def split2(v):
    hi = v.astype(BF)
    lo = (v - hi.astype(F32)).astype(BF)
    return hi, lo


def split3(v):
    hi = v.astype(BF)
    rest = v - hi.astype(F32)
    mid = rest.astype(BF)
    lo = (rest - mid.astype(F32)).astype(BF)
    return hi, mid, lo


def kernel(
    dims,
    img_ref, noise_ref, class_ref, defocus_ref, dir_ref, shift_ref, slab_ref,
    out_ref, ev_ref,
    wh, wl, cosr, sinr, csq, plain, m0, m1, grad, ra, s1, rb, s2, rc, own,
    ebuf, ta, tb, sc_acc, en_acc, use_ref, mass_ref,
    ag_s, ag_r, rs_s, rs_r, ev_s, ev_r, t_s, t_r,
):
    (X, Z, U, R, K, KC, KG) = dims
    KB = K // KC
    NI = img_ref.shape[0]
    NP = dir_ref.shape[1]
    NPOSE = 2 * U
    i = lax.axis_index("img")
    p = lax.axis_index("pose")
    z, x = lax.div(i, X), lax.rem(i, X)
    u, c = lax.div(p, 2), lax.rem(p, 2)

    def coords(off):
        dz, dx, du, dc = off
        return (lax.rem(z + dz, Z), lax.rem(x + dx, X), lax.rem(u + du, U), lax.rem(c + dc, 2))

    def device(co):
        return (co[0] * X + co[1], co[2] * 2 + co[3])

    offs_a = [(0, 0, 0, 1)]
    offs_b = [(0, dx, du, 0) for du in range(U) for dx in range(X) if du or dx]
    offs_c = [(dz, 0, 0, 0) for dz in range(1, Z)]
    offs_e = [(0, 0, du, dc) for du in range(U) for dc in range(2) if du or dc]
    offs_i = [(dz, dx, 0, 0) for dz in range(Z) for dx in range(X) if dz or dx]
    everyone = sorted(set(offs_a + offs_b + offs_c + offs_e + offs_i))
    nb, nc = len(offs_b), len(offs_c)
    per = 1 + nb + nc

    barrier = pltpu.get_barrier_semaphore()
    for off in everyone:
        pl.semaphore_signal(barrier, inc=1, device_id=device(coords(off)), device_id_type=MESH)
    pl.semaphore_wait(barrier, len(everyone))

    def send(src, dst, ss, rs, off):
        d = pltpu.make_async_remote_copy(
            src_ref=src, dst_ref=dst, send_sem=ss, recv_sem=rs,
            device_id=device(coords(off)), device_id_type=MESH,
        )
        d.start()
        return d

    pend = []

    def part(k):
        return pl.ds(k * (K // KG), K // KG)

    def gather_start(m, g):
        return [
            [
                send(m.at[c, part(k), u, x, z], m.at[c, part(k), u, x, z],
                     ag_s.at[g, k * per + n], ag_r.at[g, k * per + n], off)
                for n, off in enumerate(offs_c)
            ]
            for k in range(KG)
        ]

    def gather_b(m, g, first):
        out = []
        for k in range(KG):
            for d in first[k]:
                d.wait_recv()
            pend.extend(first[k])
            out.append([
                send(m.at[c, part(k), u, x], m.at[c, part(k), u, x],
                     ag_s.at[g, k * per + nc + n], ag_r.at[g, k * per + nc + n], off)
                for n, off in enumerate(offs_b)
            ])
        return out

    def gather_a(m, g, second):
        out = []
        for k in range(KG):
            for d in second[k]:
                d.wait_recv()
            pend.extend(second[k])
            at = k * per + nc + nb
            out.append(send(m.at[c, part(k)], m.at[c, part(k)], ag_s.at[g, at], ag_r.at[g, at], offs_a[0]))
        for d in out:
            d.wait_recv()
        pend.extend(out)

    for k in range(K):
        m0[c, k, u, x, z] = slab_ref[:, k * BW:(k + 1) * BW]
    first = gather_start(m0, 0)

    row_r = lax.broadcasted_iota(jnp.int32, (128, NI), 0)
    class_row = class_ref[...]
    hot = jnp.where(row_r % CLASSES == class_row, 1.0, 0.0)
    hot3 = jnp.where(row_r < 3 * CLASSES, hot, 0.0)
    pick = jnp.where((row_r < CLASSES) | ((row_r >= 2 * CLASSES) & (row_r < 3 * CLASSES)), hot, 0.0).astype(BF)
    hot3_t = hot3.T.astype(BF)

    srow = lax.broadcasted_iota(jnp.int32, (128, NP), 0)
    sx_ = lax.div(srow, Z * R)
    sz_ = lax.rem(lax.div(srow, R), Z)
    slab_id = jnp.where(srow < NS, (sz_ * X + sx_) * R + lax.rem(srow, R), -5)
    pdir = dir_ref[...]
    lower = lax.div(pdir, 8)
    frac = lax.rem(pdir, 8).astype(F32) / 8.0
    wt = jnp.where(slab_id == lower, 1.0 - frac, 0.0) + jnp.where(slab_id == lower + 1, frac, 0.0)
    w_t = wt[:NS].astype(BF)
    w_t2 = jnp.concatenate([w_t, w_t], axis=1)
    w = wt.T[:, :NS]
    w3 = jnp.concatenate([w, w, w], axis=1).astype(BF)

    first = gather_b(m0, 0, first)

    lane = lax.broadcasted_iota(jnp.int32, (NP, 128), 1)
    shx, shy = [
        (shift_ref[n:n + 1, :].astype(F32) + jnp.zeros((128, NP), F32)).T.astype(jnp.int32)
        for n in range(2)
    ]
    turn = 2.0 * math.pi / (4 * KH)
    base = turn * (shx * (lane % KW - KW // 2) + shy * lax.div(lane, KW)).astype(F32)
    inc = turn * (2 * shy + 0 * lane).astype(F32)
    cb, sb, ci, si = jnp.cos(base), jnp.sin(base), jnp.cos(inc), jnp.sin(inc)
    for t in range(KW * KH // 128):
        b, h = (t * 128) // BW, (t * 128) % BW
        cosr[b, :, h:h + 128] = cb
        sinr[b, :, h:h + 128] = sb
        cb, sb = cb * ci - sb * si, sb * ci + cb * si

    same = lax.broadcasted_iota(jnp.int32, (CLASSES, CLASSES), 0) == lax.broadcasted_iota(
        jnp.int32, (CLASSES, CLASSES), 1)
    blur = jnp.sum(jnp.where(same, defocus_ref[...], 0.0), axis=1, keepdims=True)
    for b in range(HB):
        pos = lax.broadcasted_iota(jnp.int32, (CLASSES, BW), 1) + b * BW
        fx = (pos % KW - KW // 2).astype(F32)
        fy = lax.div(pos, KW).astype(F32)
        rad = (fx * fx + fy * fy) / (KH * KH)
        tab = -jnp.sin(8.0 * blur * rad + 0.1)
        zero = jnp.zeros((128 - 3 * CLASSES, BW), BF)
        hi, lo = split2(tab * tab)
        csq[b] = jnp.concatenate([hi, hi, lo, zero], axis=0)
        t1, t2, t3 = split3(tab)
        sel = dot(hot3_t, jnp.concatenate([t1, t2, t3, zero], axis=0))
        for bb in (b, b + HB):
            v = sel * img_ref[:, bb * BW:(bb + 1) * BW].astype(F32)
            hi, lo = split2(v)
            wh[bb] = hi
            wl[bb] = lo
    gather_a(m0, 0, first)

    def place(b):
        q = lax.div(b, K)
        return lax.rem(q, 2), lax.rem(b, K), lax.div(q, 2)

    def rows_of(m, cc, k, uu):
        return jnp.concatenate([m[cc, k, uu, n // Z, n % Z] for n in range(X * Z)], axis=0)

    noise = noise_ref[...]

    for step in range(STEPS):
        sc_acc[...] = jnp.zeros_like(sc_acc)
        en_acc[...] = jnp.zeros_like(en_acc)

        def forward(b, carry):
            cc, k, uu = place(b)
            part = []
            for half in range(2):
                rows = rows_of(m0, cc, k, uu + half * (U // 2))
                v = dot(w3, jnp.concatenate(split3(rows), axis=0))
                plain[b + half * HB] = v
                part.append(v)
            re, im = part
            power = re * re + im * im
            hi, lo = split2(power)
            en_acc[...] += dot_t(hi, csq[b]) + dot_t(lo, csq[b])
            co, si_ = cosr[b], sinr[b]
            for half, v in enumerate((re * co - im * si_, re * si_ + im * co)):
                rh, rl = split2(v)
                bb = b + half * HB
                both = dot_t(jnp.concatenate([rh, rl], axis=0), wh[bb])
                sc_acc[...] += both[:NP] + both[NP:] + dot_t(rh, wl[bb])
            return carry

        lax.fori_loop(0, HB, forward, 0)
        e1, e2, e3 = split3(en_acc[...])
        picked = dot(e1, pick) + dot(e2, pick) + dot(e3, pick)
        scores = noise * (sc_acc[...] - 0.5 * picked)
        lpeak = jnp.max(scores, axis=0, keepdims=True)
        lsum = jnp.sum(jnp.exp(scores - lpeak), axis=0, keepdims=True)
        ebuf[step, p] = jnp.concatenate([lpeak, lsum, jnp.zeros((6, NI), F32)], axis=0)
        sent = [
            send(ebuf.at[step, p], ebuf.at[step, p], ev_s.at[step, n], ev_r.at[step, n], off)
            for n, off in enumerate(offs_e)
        ]
        for d in sent:
            d.wait()
        peak = lpeak
        for n in range(NPOSE):
            peak = jnp.maximum(peak, ebuf[step, n, 0:1, :])
        total = jnp.zeros_like(peak)
        for n in range(NPOSE):
            total += ebuf[step, n, 1:2, :] * jnp.exp(ebuf[step, n, 0:1, :] - peak)
        log_total = peak + jnp.log(total)
        usage = (noise * jnp.exp(scores - log_total)).astype(BF)
        use_ref[...] = usage
        mass = dot(usage, hot3_t)
        mh, ml = split2(mass)
        mcol = lax.broadcasted_iota(jnp.int32, mass.shape, 1)
        mass_ref[...] = jnp.where((mcol < CLASSES) | (mcol >= 2 * CLASSES), mh.astype(F32), ml.astype(F32)).astype(BF)

        def backward(cc, kc):
            def body(t, carry):
                k = kc * KB + lax.div(t, U // 2)
                uu = lax.rem(t, U // 2)
                b = (2 * uu + cc) * K + k
                use = use_ref[...]
                pr = dot(use, wh[b]) + dot(use, wl[b])
                pi = dot(use, wh[b + HB]) + dot(use, wl[b + HB])
                damp = dot(mass_ref[...], csq[b])
                co, si_ = cosr[b], sinr[b]
                outs = (
                    pr * co + pi * si_ - plain[b] * damp,
                    pi * co - pr * si_ - plain[b + HB] * damp,
                )
                for half, v in enumerate(outs):
                    hi, lo = split2(v)
                    g = dot(w_t2, jnp.concatenate([hi, lo], axis=0))
                    for n in range(X * Z):
                        grad[step, cc, k, uu + half * (U // 2), n // Z, n % Z] = g[n * R:(n + 1) * R]
                return carry

            lax.fori_loop(0, KB * (U // 2), body, 0)

        oc = lax.rem(c + 1, 2)
        stage = []
        for kc in range(KC):
            backward(oc, kc)
            ks = pl.ds(kc * KB, KB)
            stage.append(send(grad.at[step, oc, ks], ra.at[step, ks],
                              rs_s.at[step, kc * per], rs_r.at[step, kc * per], offs_a[0]))
        slot = u * X + x
        stage_b = []
        for kc in range(KC):
            backward(c, kc)
            stage[kc].wait_recv()
            ks = pl.ds(kc * KB, KB)
            for k in range(kc * KB, (kc + 1) * KB):
                s1[step, k] = grad[step, c, k] + ra[step, k]
            ds = []
            for n, off in enumerate(offs_b):
                _, xx, uu, _ = coords(off)
                ds.append(send(s1.at[step, ks, uu, xx], rb.at[step, slot, ks],
                               rs_s.at[step, kc * per + 1 + n], rs_r.at[step, kc * per + 1 + n], off))
            rb[step, slot, ks] = s1[step, ks, u, x]
            stage_b.append(ds)
        stage_c = []
        for kc in range(KC):
            for d in stage_b[kc]:
                d.wait_recv()
            ks = pl.ds(kc * KB, KB)
            tot = rb[step, 0, ks]
            for n in range(1, U * X):
                tot += rb[step, n, ks]
            s2[step, ks] = tot
            ds = []
            for n, off in enumerate(offs_c):
                zz = coords(off)[0]
                ds.append(send(s2.at[step, ks, zz], rc.at[step, z, ks],
                               rs_s.at[step, kc * per + 1 + nb + n], rs_r.at[step, kc * per + 1 + nb + n], off))
            rc[step, z, ks] = s2[step, ks, z]
            stage_c.append(ds)
        for kc in range(KC):
            for d in stage_c[kc]:
                d.wait_recv()
            ks = pl.ds(kc * KB, KB)
            tot = rc[step, 0, ks]
            for n in range(1, Z):
                tot += rc[step, n, ks]
            own[ks] = tot
        pend.extend(stage)
        for ds in stage_b + stage_c:
            pend.extend(ds)

        if step < STEPS - 1:
            m1[c, :, u, x, z] = own[...]
            first = gather_start(m1, 1)
            first = gather_b(m1, 1, first)
            gather_a(m1, 1, first)
            sq = jnp.zeros((R, BW), F32)
            for cc in range(2):
                for k in range(K):
                    for uu in range(U):
                        for n in range(X * Z):
                            v = m1[cc, k, uu, n // Z, n % Z]
                            sq += v * v
            spread = jnp.sqrt(jnp.sum(sq, keepdims=True) / (NS * F) + 1e-06)
            for d in pend:
                d.wait_send()
            pend.clear()
            for cc in range(2):
                for k in range(K):
                    for uu in range(U):
                        for n in range(X * Z):
                            at = (cc, k, uu, n // Z, n % Z)
                            m0[at] = m0[at] + 0.05 * m1[at] / spread
        else:
            g = own[...]
            mine = jnp.sum(jnp.sum(g * g, axis=0), keepdims=True)
            ta[p] = mine + jnp.zeros((8, 128), F32)
            ds = [send(ta.at[p], ta.at[p], t_s.at[n], t_r.at[n], off) for n, off in enumerate(offs_e)]
            for d in ds:
                d.wait()
            tot = ta[0]
            for n in range(1, NPOSE):
                tot += ta[n]
            tb[i] = tot
            ds = [send(tb.at[i], tb.at[i], t_s.at[NPOSE + n], t_r.at[NPOSE + n], off) for n, off in enumerate(offs_i)]
            for d in ds:
                d.wait()
            tot = tb[0]
            for n in range(1, X * Z):
                tot += tb[n]
            spread = jnp.sqrt(tot[0:1, 0:1] / (NS * F) + 1e-06)
            for k in range(K):
                out_ref[:, k * BW:(k + 1) * BW] = m0[c, k, u, x, z] + 0.05 * own[k] / spread
            share = NI // NPOSE
            ev = jnp.zeros((1, share), F32)
            for n in range(NPOSE):
                ev = jnp.where(p == n, log_total[:, n * share:(n + 1) * share], ev)
            ev_ref[...] = ev
    for d in pend:
        d.wait_send()


def shards(dims, images, inv_noise, defocus_class, defocus, pose_dir, pose_shift, slabs):
    X, Z, U, R, K, KC, KG = dims
    ni, np_ = images.shape[0], pose_dir.shape[0]
    C = slabs.shape[1]
    npose = 2 * U
    nb, nc = U * X - 1, Z - 1
    vm = pltpu.VMEM
    dma = pltpu.SemaphoreType.DMA
    whole = (2, K, U, X, Z, R, BW)
    per = 1 + nb + nc
    scratch = [
        vm((NB, ni, BW), BF), vm((NB, ni, BW), BF),
        vm((HB, np_, BW), F32), vm((HB, np_, BW), F32),
        vm((HB, 128, BW), BF),
        vm((NB, np_, BW), F32),
        vm(whole, F32), vm(whole, F32),
        vm((STEPS,) + whole, F32),
        vm((STEPS,) + whole[1:], F32), vm((STEPS,) + whole[1:], F32),
        vm((STEPS, U * X, K, Z, R, BW), F32),
        vm((STEPS, K, Z, R, BW), F32),
        vm((STEPS, Z, K, R, BW), F32),
        vm((K, R, BW), F32),
        vm((STEPS, npose, 8, ni), F32),
        vm((npose, 8, 128), F32), vm((X * Z, 8, 128), F32),
        vm((np_, ni), F32), vm((np_, 128), F32),
        vm((np_, ni), BF), vm((np_, 128), BF),
        dma((2, KG * per)), dma((2, KG * per)),
        dma((STEPS, KC * per)), dma((STEPS, KC * per)),
        dma((STEPS, npose)), dma((STEPS, npose)),
        dma((npose + X * Z,)), dma((npose + X * Z,)),
    ]
    out, ev = pl.pallas_call(
        functools.partial(kernel, dims),
        out_shape=(
            jax.ShapeDtypeStruct(slabs.shape, F32),
            jax.ShapeDtypeStruct((1, ni // npose), F32),
        ),
        in_specs=[pl.BlockSpec(memory_space=vm)] * 7,
        out_specs=(pl.BlockSpec(memory_space=vm),) * 2,
        scratch_shapes=scratch,
        compiler_params=pltpu.CompilerParams(
            collective_id=0, has_side_effects=True, vmem_limit_bytes=56 * 1024 * 1024
        ),
        cost_estimate=pl.CostEstimate(flops=8 * ni * np_ * F, bytes_accessed=2 * ni * F, transcendentals=0),
    )(
        images, inv_noise[None, :], defocus_class[None, :], defocus[None, :],
        pose_dir[None, :], pose_shift.T, slabs,
    )
    return out, ev[0]


def solution(mesh):
    n_img, n_pose = mesh.shape["img"], mesh.shape["pose"]
    X, Z, U = 2, n_img // 2, n_pose // 2
    R = NS // n_img
    K = F // n_pose // BW
    KC = K
    KG = 2 if K % 2 == 0 else 1
    in_specs = (
        P("img", None),
        P("img"),
        P("img"),
        P(),
        P("pose"),
        P("pose", None),
        P("img", "pose"),
    )
    out_specs = (P("img", "pose"), P(("img", "pose")))
    body = functools.partial(shards, (X, Z, U, R, K, KC, KG))
    return jax.shard_map(body, mesh=mesh, in_specs=in_specs, out_specs=out_specs, check_vma=False)
```
